512 devices in a mesh: pool: 4 (over x), ep: 128 (over y, z, core).
Axes of the slice: x: 4, y: 8, z: 8, core: 2. Of those that a mesh axis runs over, the one named last changes fastest.
Arguments:
- kv_pre: bfloat16 [262144, 576], P(('pool', 'ep')), may hold values from -6 to 6
- kv_gain: float32 [512], replicated, may hold values from 0.5 to 2
- send_list: int32 [512, 512, 1], P(('pool', 'ep')), may hold values from 0 to 511, as said below
- row_owner: int32 [262144], P(('pool', 'ep')), may hold values from 0 to 1
- queries: bfloat16 [1024, 128, 576], P(('pool', 'ep')), may hold values from -12 to 12
- cache: bfloat16 [1024, 1024, 576], P(('pool', 'ep')), may hold values from -4 to 4
- ctx_len: int32 [1024], P(('pool', 'ep')), may hold values from 2 to 1024, as said below
- value_up: bfloat16 [128, 512, 128], P('ep'), may hold values from -1.5 to 1.5
Outputs:
- head_values: bfloat16 [1024, 128, 128], P(('pool', 'ep'))
The draws below stay inside these ranges and needn't reach their ends.
Inputs may be any that keep to these rules, and one draw needn't show every extreme that they name: For each source device s, the entries send_list[s, :, :] name each of its 512 prompt rows exactly once; every slot is filled. `ctx_len`: some row reaches 1024.
All inputs are finite; a program needn't handle non-finite values.
Results may differ from the reference program's by a relative error of at most 0.014.
Values may be sent and summed in bfloat16 or wider, within the bound.
A program may use at most 64 MiB of HBM per device.

```python
import math
import jax
import jax.numpy as jnp
from jax import lax

H = 128
LAT = 512
ROPE = 64
VHEAD = 128
PRE = 512
ROWS = 2
CACHE = 1024
NODES = 512
CAP = 1
TOKENS = 262144
DEC = 1024


def draw_cache(key, part):
    key = jax.random.fold_in(key, 21)
    base = jnp.clip(jax.random.normal(key, (DEC, CACHE, LAT + ROPE), jnp.float32), -4.0, 4.0)
    return base.astype(jnp.bfloat16)


def draw_queries(key, part):
    key = jax.random.fold_in(key, 22)
    base = jnp.clip(jax.random.normal(key, (DEC, H, LAT + ROPE), jnp.float32), -4.0, 4.0)
    return base.astype(jnp.bfloat16)


def draw_ctx_len(key, part):
    key = jax.random.fold_in(key, 31)
    left_key, right_key, long_key = jax.random.split(key, 3)
    left_part = jax.random.randint(left_key, (DEC,), 0, CACHE - 1, jnp.int32)
    right_part = jax.random.randint(right_key, (DEC,), 0, CACHE - 1, jnp.int32)
    lengths = 2 + left_part * right_part // (CACHE - 1)
    longest = jax.random.randint(long_key, (), 0, DEC, jnp.int32)
    return lengths.at[longest].set(CACHE).astype(jnp.int32)


def draw_row_owner(key, part):
    key = jax.random.fold_in(key, 51)
    owners = jax.random.randint(key, (TOKENS,), 0, ROWS, jnp.int32)
    owners = owners.at[0].set(0).at[1].set(ROWS - 1)
    return owners.astype(jnp.int32)


def draw_send_list(key, part):
    key = jax.random.fold_in(key, 41)

    def one_source(source_key):
        order = jax.random.permutation(source_key, PRE).astype(jnp.int32)
        return order.reshape(NODES, CAP)
    return jax.vmap(one_source)(jax.random.split(key, NODES)).astype(jnp.int32)


def steps_of(stream_key, extent, shards, low, top_value):
    level = 1.0
    for axis_at, blocks in shards:
        steps = jax.random.uniform(jax.random.fold_in(jax.random.fold_in(stream_key, 6), axis_at), (blocks,), jnp.float32, low / len(shards), top_value / len(shards))
        level = level * jnp.repeat(jnp.exp(steps), extent[axis_at] // blocks).reshape((-1,) + (1,) * (len(extent) - 1 - axis_at))
    return level


def gaussian(stream_key, extent, deviation, limit, cuts=(), held_as=jnp.bfloat16):
    loudness = steps_of(stream_key, extent, cuts, -0.22, 0.18) if cuts else 1.0
    array = jax.random.normal(stream_key, extent, jnp.float32) * deviation * loudness
    return jnp.minimum(jnp.maximum(array, -limit), limit).astype(held_as)


def setup_inputs(seed: int = 0) -> dict:
    keys = jax.random.split(jax.random.key(seed), 9)
    return {
        "kv_pre": gaussian(keys[0], (TOKENS, LAT + ROPE), 1.0, 6.0, ((0, 512),)),
        "kv_gain": jnp.clip(jnp.exp(jax.random.uniform(keys[1], (LAT,), jnp.float32, math.log(0.5), math.log(2.0))), 0.5, 2.0),
        "send_list": draw_send_list(jax.random.fold_in(keys[8], 71), 0),
        "row_owner": draw_row_owner(jax.random.fold_in(keys[8], 71), 0),
        "queries": draw_queries(jax.random.fold_in(keys[8], 71), 0),
        "cache": draw_cache(jax.random.fold_in(keys[8], 71), 0),
        "ctx_len": draw_ctx_len(jax.random.fold_in(keys[8], 71), 0),
        "value_up": gaussian(keys[7], (H, LAT, VHEAD), 16 ** -0.5, 1.5, ((0, 128),)),
    }


score_scale = 192.0 ** (-0.5)
epsilon = 1e-06

def prefill_rows(kv_pre, kv_gain, row_start):
    values = kv_pre.astype(jnp.float32)
    lat_width = kv_gain.shape[0]
    latent = values[:, :lat_width]
    mean_square = lax.optimization_barrier(jnp.mean(latent * latent, axis=-1, keepdims=True))
    normed = latent * lax.rsqrt(mean_square + epsilon) * kv_gain
    rotary = values[:, lat_width:]
    half_width = rotary.shape[1] // 2
    position = (row_start + jnp.arange(values.shape[0], dtype=jnp.int32)).astype(jnp.float32)
    frequency = 10000.0 ** (-jnp.arange(half_width, dtype=jnp.float32) / half_width)
    angles = position[:, None] * frequency[None, :]
    first_half = rotary[:, :half_width]
    second = rotary[:, half_width:]
    cosine = jnp.cos(angles)
    sine_part = jnp.sin(angles)
    return jnp.concatenate([normed, first_half * cosine - second * sine_part, first_half * sine_part + second * cosine], axis=1).astype(jnp.bfloat16)

def attend(query, cache_rows, lengths, fresh_rows, owner_row, lat_width):
    row_count = query.shape[0]
    query32 = query.astype(jnp.float32)
    cache32 = cache_rows.astype(jnp.float32)
    fresh32 = fresh_rows.astype(jnp.float32)
    score_cache = jnp.einsum('rhw,rkw->rhk', query32, cache32) * score_scale
    score_fresh = jnp.einsum('rhw,kw->rhk', query32, fresh32) * score_scale
    live_cache = jnp.arange(cache_rows.shape[1], dtype=jnp.int32)[None, None, :] < lengths[:, None, None]
    live_fresh = owner_row[None, None, :] == jnp.arange(row_count, dtype=jnp.int32)[:, None, None]
    score_cache = jnp.where(live_cache, score_cache, -jnp.inf)
    score_fresh = jnp.where(live_fresh, score_fresh, -jnp.inf)
    peak = jnp.maximum(lax.optimization_barrier(jnp.max(score_cache, axis=-1, keepdims=True)), lax.optimization_barrier(jnp.max(score_fresh, axis=-1, keepdims=True)))
    weight_cache = jnp.exp(score_cache - peak)
    weight_fresh = jnp.exp(score_fresh - peak)
    denominator = lax.optimization_barrier(jnp.sum(weight_cache, axis=-1, keepdims=True)) + lax.optimization_barrier(jnp.sum(weight_fresh, axis=-1, keepdims=True))
    prob_cache = (weight_cache / denominator).astype(jnp.bfloat16).astype(jnp.float32)
    prob_fresh = (weight_fresh / denominator).astype(jnp.bfloat16).astype(jnp.float32)
    summed = jnp.einsum('rhk,rkl->rhl', prob_cache, cache32[..., :lat_width])
    summed = summed + jnp.einsum('rhk,kl->rhl', prob_fresh, fresh32[:, :lat_width])
    return summed.astype(jnp.bfloat16)

def reference(kv_pre, kv_gain, send_list, row_owner, queries, cache, ctx_len, value_up):
    latent_rows = prefill_rows(kv_pre, kv_gain, 0)

    def one_device(device):
        send_slots = lax.dynamic_index_in_dim(send_list, device, 1, keepdims=False)
        filled = send_slots >= 0
        global_row = (jnp.arange(NODES, dtype=jnp.int32)[:, None] * PRE + jnp.maximum(send_slots, 0)).astype(jnp.int32)
        fresh_rows = jnp.where(filled[:, :, None], latent_rows[global_row], jnp.zeros((), jnp.bfloat16))
        fresh_rows = fresh_rows.reshape(NODES * CAP, LAT + ROPE)
        owner_row = jnp.where(filled, row_owner[global_row], -1).reshape(NODES * CAP).astype(jnp.int32)
        first_row = (device * ROWS).astype(jnp.int32)
        query = lax.dynamic_slice_in_dim(queries, first_row, ROWS, 0)
        cache_rows = lax.dynamic_slice_in_dim(cache, first_row, ROWS, 0)
        lengths = lax.dynamic_slice_in_dim(ctx_len, first_row, ROWS, 0)
        return attend(query, cache_rows, lengths, fresh_rows, owner_row, LAT)
    attended = lax.map(one_device, jnp.arange(NODES, dtype=jnp.int32)).reshape(DEC, H, LAT)
    projected = jnp.einsum('rhl,hlv->rhv', attended.astype(jnp.float32), value_up.astype(jnp.float32))
    return projected.astype(jnp.bfloat16)
```

```python
import functools
import math

import jax
import jax.numpy as jnp
import numpy as np
from jax import lax
from jax.experimental import pallas as pl
from jax.experimental.pallas import tpu as pltpu
from jax.sharding import PartitionSpec as P

MESH = pl.DeviceIdType.MESH
score_scale = 192.0 ** (-0.5)
epsilon = 1e-06
f32 = jnp.float32
bf16 = jnp.bfloat16
masked = -1e30


def far_first(step, size):
    return size // 2 + ((step + 1) // 2) * (1 - 2 * (step % 2))


def dot_nn(a, b):
    return jnp.dot(a, b, preferred_element_type=f32)


def dot_nt(a, b):
    return lax.dot_general(a, b, (((1,), (1,)), ((), ())), preferred_element_type=f32)


def iota(shape, dim):
    return lax.broadcasted_iota(jnp.int32, shape, dim)


def one_hot(condition):
    return jnp.where(condition, 1.0, 0.0).astype(bf16)


def kernel(
    nx, ny, nz, lat, rope,
    freq_ref, gain_ref, send_ref, owner_ref, len_ref,
    kv_hbm, query_hbm, cache_hbm, value_hbm,
    out_ref,
    kv, query_t, cache, value, qpad, core_out, core_in,
    msg1, got1, msg2, got2, msg3, got3,
    load_sem, core_send, core_recv, val_send, val_recv,
    send1, recv1, send2, recv2, send3, recv3, plane_sem,
):
    x = lax.axis_index("pool")
    ep = lax.axis_index("ep")
    y = ep // (2 * nz)
    z = (ep % (2 * nz)) // 2
    core = ep % 2
    chip = (x * ny + y) * nz + z
    place = y * nz + z
    chips = nx * ny * nz
    places = ny * nz
    prompt = kv.shape[1]
    width = lat + rope
    padded = kv.shape[0]
    heads = query_t.shape[2]
    half = rope // 2
    partner = (x, ep + 1 - 2 * core)

    def device(cx, cy, cz):
        return (cx, (cy * nz + cz) * 2 + core)

    barrier = pltpu.get_barrier_semaphore()

    def greet_plane(step, carry):
        cx = (x + step // ny) % nx
        cy = (y + step % ny) % ny
        pl.semaphore_signal(barrier, inc=1, device_id=device(cx, cy, z), device_id_type=MESH)
        return carry

    def greet_ring(step, carry):
        pl.semaphore_signal(
            barrier, inc=1, device_id=device(x, y, (z + step) % nz), device_id_type=MESH
        )
        return carry

    lax.fori_loop(1, nx * ny, greet_plane, 0)
    lax.fori_loop(1, nz, greet_ring, 0)
    pl.semaphore_signal(barrier, inc=1, device_id=partner, device_id_type=MESH)

    load_kv = pltpu.make_async_copy(kv_hbm, kv.at[pl.ds(0, width)], load_sem.at[0])
    load_value = pltpu.make_async_copy(value_hbm.at[0], value.at[core], load_sem.at[1])
    load_query = pltpu.make_async_copy(query_hbm, query_t, load_sem.at[2])
    load_cache = pltpu.make_async_copy(cache_hbm, cache, load_sem.at[3])
    load_kv.start()
    load_value.start()
    load_query.start()
    load_cache.start()

    send_row = send_ref[...].astype(f32)
    lane = iota((chips, prompt), 1)
    line = iota((chips, prompt), 0)
    send_other = jnp.sum(
        jnp.where(lane == 2 * line + (1 - core), send_row, 0.0), axis=1, keepdims=True
    )
    wide_lane = iota((2 * chips, prompt), 1)
    wide_line = iota((2 * chips, prompt), 0)
    send_own = jnp.sum(jnp.where(wide_lane == wide_line, send_row, 0.0), axis=1, keepdims=True)
    pick_other = one_hot(lane.astype(f32) == send_other)
    pick_own = one_hot(
        jnp.logical_and(wide_lane.astype(f32) == send_own, wide_line % 2 == core)
    )

    first_row = ((x * ny + y) * nz + z) * 2 + core
    position = (first_row * prompt + iota((half, prompt), 1)).astype(f32)
    angles = position * freq_ref[...]
    turns = jnp.floor(angles * (1.0 / (2.0 * math.pi)) + 0.5)
    angles = ((angles - turns * 6.28125) - turns * 0.0019340515136718750) - turns * 1.2556659146e-06
    cosine = jnp.cos(angles)
    sine = jnp.sin(angles)
    load_kv.wait()
    first = kv[lat : lat + half, :].astype(f32)
    second = kv[lat + half : width, :].astype(f32)
    kv[lat : lat + half, :] = (first * cosine - second * sine).astype(bf16)
    kv[lat + half : width, :] = (first * sine + second * cosine).astype(bf16)
    tail = padded - width
    kv[width:padded, :] = jnp.where(
        iota((tail, prompt), 0) == 0, owner_ref[...].astype(f32), 0.0
    ).astype(bf16)

    def rows_of(pick):
        picked = dot_nt(pick, kv[...])
        latent = picked[:, :lat]
        mean_square = jnp.mean(latent * latent, axis=1, keepdims=True)
        normed = latent * lax.rsqrt(mean_square + epsilon) * gain_ref[...]
        return jnp.concatenate([normed, picked[:, lat:]], axis=1).astype(bf16)

    core_out[...] = rows_of(pick_other)

    pl.semaphore_wait(barrier, nx * ny - 1 + nz - 1 + 1)

    def plane_ready(step, carry):
        pl.semaphore_signal(
            plane_sem, inc=1, device_id=device(x, y, (z + step) % nz), device_id_type=MESH
        )
        return carry

    lax.fori_loop(1, nz, plane_ready, 0)
    swap = pltpu.make_async_remote_copy(
        src_ref=core_out, dst_ref=core_in, send_sem=core_send, recv_sem=core_recv,
        device_id=partner, device_id_type=MESH,
    )
    swap.start()
    load_value.wait()
    swap_value = pltpu.make_async_remote_copy(
        src_ref=value.at[core], dst_ref=value.at[core], send_sem=val_send, recv_sem=val_recv,
        device_id=partner, device_id_type=MESH,
    )
    swap_value.start()

    own_rows = rows_of(pick_own)
    spread = one_hot(iota((2 * chips, chips), 0) == 2 * iota((2 * chips, chips), 1) + (1 - core))
    swap.wait()
    both = own_rows.astype(f32) + dot_nn(spread, core_in[...])
    msg1[...] = both.astype(bf16).reshape(chips, 2, padded)

    pl.semaphore_wait(plane_sem, nz - 1)

    def send_rows(step, carry):
        cx = (x + far_first(step // places, nx)) % nx
        cy = (y + far_first((step // nz) % ny, ny)) % ny
        cz = (z + far_first(step % nz, nz)) % nz
        pltpu.make_async_remote_copy(
            src_ref=msg1.at[(cx * ny + cy) * nz + cz], dst_ref=got1.at[chip],
            send_sem=send1, recv_sem=recv1, device_id=device(cx, cy, cz), device_id_type=MESH,
        ).start()
        return carry

    lax.fori_loop(0, chips - 1, send_rows, 0)
    got1[pl.ds(chip, 1)] = msg1[pl.ds(chip, 1)]

    load_query.wait()
    unit = one_hot(iota((heads, heads), 0) == iota((heads, heads), 1))
    for r in range(2):
        qpad[r * heads : (r + 1) * heads, :] = jnp.concatenate(
            [dot_nt(unit, query_t[r]), jnp.zeros((heads, tail), f32)], axis=1
        ).astype(bf16)
    qpad[2 * heads : 2 * heads + 16, :] = one_hot(
        jnp.logical_and(iota((16, padded), 0) == 0, iota((16, padded), 1) == width)
    )

    load_cache.wait()
    peaks, sums, totals = [], [], []
    for r in range(2):
        scores = dot_nn(qpad[r * heads : (r + 1) * heads, :width], cache[r]) * score_scale
        scores = jnp.where(iota(scores.shape, 1) < len_ref[r], scores, masked)
        peak = jnp.max(scores, axis=1, keepdims=True)
        weight = jnp.exp(scores - peak)
        peaks.append(peak)
        sums.append(jnp.sum(weight, axis=1, keepdims=True))
        totals.append(dot_nt(weight.astype(bf16), cache[r, :lat, :]))
    peak_cache = jnp.concatenate(peaks, axis=0)
    sum_cache = jnp.concatenate(sums, axis=0)
    total_cache = jnp.concatenate(totals, axis=0)

    all_rows = pltpu.make_async_copy(
        msg1.at[pl.ds(0, chips - 1)], got1.at[pl.ds(0, chips - 1)], recv1
    )
    all_rows.wait()
    fresh = got1[...].reshape(2 * chips, padded)
    raw = dot_nt(qpad[...], fresh)
    owner = raw[2 * heads : 2 * heads + 1, :]
    scores = raw[: 2 * heads, :] * score_scale
    row = (iota(scores.shape, 0) // heads).astype(f32)
    scores = jnp.where(row == owner, scores, masked)
    peak = jnp.maximum(peak_cache, jnp.max(scores, axis=1, keepdims=True))
    weight = jnp.exp(scores - peak)
    scale_cache = jnp.exp(peak_cache - peak)
    denominator = sum_cache * scale_cache + jnp.sum(weight, axis=1, keepdims=True)
    total = total_cache * scale_cache + dot_nn(weight.astype(bf16), fresh[:, :lat])
    attended = (total / denominator).astype(bf16)

    line = iota((2 * heads, 2 * heads), 0)
    lane = iota((2 * heads, 2 * heads), 1)
    by_chip = one_hot(lane == ((line // 2) % 2) * heads + (line // 4) * 2 + line % 2)
    msg2[...] = dot_nn(by_chip, attended).astype(bf16).reshape(places, 4, lat)

    def send_heads(step, carry):
        cy = (y + far_first(step // nz, ny)) % ny
        cz = (z + far_first(step % nz, nz)) % nz
        pltpu.make_async_remote_copy(
            src_ref=msg2.at[cy * nz + cz], dst_ref=got2.at[place],
            send_sem=send2, recv_sem=recv2, device_id=device(x, cy, cz), device_id_type=MESH,
        ).start()
        return carry

    lax.fori_loop(0, places - 1, send_heads, 0)
    got2[pl.ds(place, 1)] = msg2[pl.ds(place, 1)]
    swap_value.wait()
    weights = jnp.concatenate([value[0], value[1]], axis=1)
    pltpu.make_async_copy(
        msg2.at[pl.ds(0, places - 1)], got2.at[pl.ds(0, places - 1)], recv2
    ).wait()
    vhead = value.shape[2]
    projected = dot_nn(got2[...].reshape(4 * places, lat), weights)
    even = iota((4 * places, vhead), 0) % 2 == 0
    mine = jnp.where(even, projected[:, :vhead], projected[:, vhead:])
    msg3[...] = mine.astype(bf16).reshape(places, 4, vhead)

    def send_back(step, carry):
        cy = (y + far_first(step // nz, ny)) % ny
        cz = (z + far_first(step % nz, nz)) % nz
        pltpu.make_async_remote_copy(
            src_ref=msg3.at[cy * nz + cz], dst_ref=got3.at[place],
            send_sem=send3, recv_sem=recv3, device_id=device(x, cy, cz), device_id_type=MESH,
        ).start()
        return carry

    lax.fori_loop(0, places - 1, send_back, 0)
    got3[pl.ds(place, 1)] = msg3[pl.ds(place, 1)]
    by_row = one_hot(line == ((lane // 2) % 2) * heads + (lane // 4) * 2 + lane % 2)
    pltpu.make_async_copy(
        msg3.at[pl.ds(0, places - 1)], got3.at[pl.ds(0, places - 1)], recv3
    ).wait()
    out_ref[...] = (
        dot_nn(by_row, got3[...].reshape(4 * places, vhead)).astype(bf16).reshape(2, heads, vhead)
    )

    pltpu.make_async_copy(
        msg1.at[pl.ds(0, chips - 1)], got1.at[pl.ds(0, chips - 1)], send1
    ).wait()
    pltpu.make_async_copy(
        msg2.at[pl.ds(0, places - 1)], got2.at[pl.ds(0, places - 1)], send2
    ).wait()
    pltpu.make_async_copy(
        msg3.at[pl.ds(0, places - 1)], got3.at[pl.ds(0, places - 1)], send3
    ).wait()


def body(kv_pre, kv_gain, send_list, row_owner, queries, cache, ctx_len, value_up):
    nx = lax.axis_size("pool")
    places = lax.axis_size("ep") // 2
    ny = nz = math.isqrt(places)
    chips = nx * places
    lat = kv_gain.shape[0]
    width = kv_pre.shape[1]
    rope = width - lat
    prompt = kv_pre.shape[0]
    rows, heads, _ = queries.shape
    slots = cache.shape[1]
    vhead = value_up.shape[2]
    padded = -(-(width + 1) // 128) * 128
    half = rope // 2
    frequency = np.float32(10000.0) ** (-np.arange(half, dtype=np.float32) / np.float32(half))
    frequency = np.broadcast_to(frequency.astype(np.float32)[:, None], (half, prompt))

    vmem = pl.BlockSpec(memory_space=pltpu.VMEM)
    smem = pl.BlockSpec(memory_space=pltpu.SMEM)
    hbm = pl.BlockSpec(memory_space=pl.ANY)
    dma = pltpu.SemaphoreType.DMA
    return pl.pallas_call(
        functools.partial(kernel, nx, ny, nz, lat, rope),
        out_shape=jax.ShapeDtypeStruct((rows, heads, vhead), bf16),
        in_specs=[vmem, vmem, vmem, vmem, smem, hbm, hbm, hbm, hbm],
        out_specs=vmem,
        scratch_shapes=[
            pltpu.VMEM((padded, prompt), bf16),
            pltpu.VMEM((rows, width, heads), bf16),
            pltpu.VMEM((rows, width, slots), bf16),
            pltpu.VMEM((2, lat, vhead), bf16),
            pltpu.VMEM((rows * heads + 16, padded), bf16),
            pltpu.VMEM((chips, padded), bf16),
            pltpu.VMEM((chips, padded), bf16),
            pltpu.VMEM((chips, 2, padded), bf16),
            pltpu.VMEM((chips, 2, padded), bf16),
            pltpu.VMEM((places, 4, lat), bf16),
            pltpu.VMEM((places, 4, lat), bf16),
            pltpu.VMEM((places, 4, vhead), bf16),
            pltpu.VMEM((places, 4, vhead), bf16),
            dma((4,)),
            dma, dma, dma, dma,
            dma, dma, dma, dma, dma, dma,
            pltpu.SemaphoreType.REGULAR,
        ],
        compiler_params=pltpu.CompilerParams(
            collective_id=0, has_side_effects=True, vmem_limit_bytes=56 * 2**20
        ),
        name="serve_window",
    )(
        jnp.asarray(frequency),
        kv_gain.reshape(1, lat),
        send_list.reshape(1, prompt),
        row_owner.reshape(1, prompt),
        ctx_len,
        kv_pre.T,
        queries.transpose(0, 2, 1),
        cache.transpose(0, 2, 1),
        value_up,
    )


def solution(mesh):
    in_specs = (
        P(("pool", "ep"), None),
        P(),
        P(("pool", "ep"), None, None),
        P(("pool", "ep")),
        P(("pool", "ep"), None, None),
        P(("pool", "ep"), None, None),
        P(("pool", "ep")),
        P("ep", None, None),
    )
    out_specs = P(("pool", "ep"), None, None)
    return jax.shard_map(body, mesh=mesh, in_specs=in_specs, out_specs=out_specs, check_vma=False)
```

```python
import functools
import math

import jax
import jax.numpy as jnp
import numpy as np
from jax import lax
from jax.experimental import pallas as pl
from jax.experimental.pallas import tpu as pltpu
from jax.sharding import PartitionSpec as P

MESH = pl.DeviceIdType.MESH
score_scale = 192.0 ** (-0.5)
epsilon = 1e-06
f32 = jnp.float32
bf16 = jnp.bfloat16
masked = -1e30


def far_first(step, size):
    if isinstance(step, int):
        return size // 2 + ((step + 1) // 2) * (1 - 2 * (step % 2))
    return size // 2 + lax.div(step + 1, 2) * (1 - 2 * lax.rem(step, 2))


def moved(position, step, size):
    place = position + far_first(step, size)
    return jnp.where(place >= size, place - size, place)


def dot_nn(a, b):
    return jnp.dot(a, b, preferred_element_type=f32)


def dot_nt(a, b):
    return lax.dot_general(a, b, (((1,), (1,)), ((), ())), preferred_element_type=f32)


def iota(shape, dim):
    return lax.broadcasted_iota(jnp.int32, shape, dim)


def one_hot(condition):
    return jnp.where(condition, 1.0, 0.0).astype(bf16)


def kernel(
    nx, ny, nz, lat, rope,
    gain_hbm, send_hbm, owner_hbm, len_hbm, kv_hbm, query_hbm, cache_hbm, value_hbm,
    out_ref,
    gain_ref, send_ref, owner_ref, len_ref, kv, query_t, cache, value, qpad, core_out, core_in,
    msg1, got1, msg2, got2, msg3, got3,
    load_sem, core_send, core_recv, val_send, val_recv,
    send1, recv1, send2, recv2, send3, recv3, plane_sem,
):
    x = lax.axis_index("pool")
    ep = lax.axis_index("ep")
    y = lax.div(ep, 2 * nz)
    z = lax.div(lax.rem(ep, 2 * nz), 2)
    core = lax.rem(ep, 2)
    chip = (x * ny + y) * nz + z
    place = y * nz + z
    chips = nx * ny * nz
    places = ny * nz
    prompt = kv.shape[1]
    width = lat + rope
    padded = kv.shape[0]
    heads = query_t.shape[2]
    half = rope // 2
    partner = (x, ep + 1 - 2 * core)

    def device(cx, cy, cz):
        return (cx, (cy * nz + cz) * 2 + core)

    barrier = pltpu.get_barrier_semaphore()

    far_y = [moved(y, step, ny) for step in range(ny - 1)]
    far_z = [moved(z, step, nz) for step in range(nz - 1)]

    def greet(cx, cy, cz):
        pl.semaphore_signal(barrier, inc=1, device_id=device(cx, cy, cz), device_id_type=MESH)

    def greet_plane(step, carry):
        cx = moved(x, step, nx)
        for cy in far_y + [y]:
            greet(cx, cy, z)
        return carry

    lax.fori_loop(0, nx - 1, greet_plane, 0)
    for cy in far_y:
        greet(x, cy, z)
    for cz in far_z:
        greet(x, y, cz)
    pl.semaphore_signal(barrier, inc=1, device_id=partner, device_id_type=MESH)

    load_kv = pltpu.make_async_copy(kv_hbm, kv.at[pl.ds(0, width)], load_sem.at[0])
    load_value = pltpu.make_async_copy(value_hbm.at[0], value.at[core], load_sem.at[1])
    load_query = pltpu.make_async_copy(query_hbm, query_t, load_sem.at[2])
    load_cache = pltpu.make_async_copy(cache_hbm, cache, load_sem.at[3])
    load_gain = pltpu.make_async_copy(gain_hbm, gain_ref, load_sem.at[4])
    load_send = pltpu.make_async_copy(send_hbm, send_ref, load_sem.at[5])
    load_owner = pltpu.make_async_copy(owner_hbm, owner_ref, load_sem.at[6])
    load_len = pltpu.make_async_copy(len_hbm, len_ref, load_sem.at[7])
    load_send.start()
    load_kv.start()
    load_owner.start()
    load_gain.start()
    load_len.start()
    load_value.start()
    load_query.start()
    load_cache.start()

    load_send.wait()
    send_row = send_ref[...].astype(f32)
    lane = iota((chips, prompt), 1)
    line = iota((chips, prompt), 0)
    send_other = jnp.sum(
        jnp.where(lane == 2 * line + (1 - core), send_row, 0.0), axis=1, keepdims=True
    )
    wide_lane = iota((2 * chips, prompt), 1)
    wide_line = iota((2 * chips, prompt), 0)
    send_own = jnp.sum(jnp.where(wide_lane == wide_line, send_row, 0.0), axis=1, keepdims=True)
    pick_other = one_hot(lane.astype(f32) == send_other)
    pick_own = one_hot(
        jnp.logical_and(wide_lane.astype(f32) == send_own, wide_line % 2 == core)
    )

    first_row = ((x * ny + y) * nz + z) * 2 + core
    position = (first_row * prompt + iota((half, prompt), 1)).astype(f32)
    index = iota((half, prompt), 0)
    frequency = jnp.zeros((half, prompt), f32)
    for j in range(half):
        frequency = jnp.where(index == j, float(np.float32(10000.0 ** (-j / half))), frequency)
    angles = position * frequency
    turns = jnp.floor(angles * (1.0 / (2.0 * math.pi)) + 0.5)
    angles = ((angles - turns * 6.28125) - turns * 0.0019340515136718750) - turns * 1.2556659146e-06
    cosine = jnp.cos(angles)
    sine = jnp.sin(angles)
    load_kv.wait()
    first = kv[lat : lat + half, :].astype(f32)
    second = kv[lat + half : width, :].astype(f32)
    kv[lat : lat + half, :] = (first * cosine - second * sine).astype(bf16)
    kv[lat + half : width, :] = (first * sine + second * cosine).astype(bf16)
    tail = padded - width
    load_owner.wait()
    kv[width:padded, :] = jnp.where(
        iota((tail, prompt), 0) == 0, owner_ref[...].astype(f32), 0.0
    ).astype(bf16)

    def rows_of(pick):
        picked = dot_nt(pick, kv[...])
        latent = picked[:, :lat]
        mean_square = jnp.mean(latent * latent, axis=1, keepdims=True)
        normed = latent * lax.rsqrt(mean_square + epsilon) * gain_ref[...]
        return jnp.concatenate([normed, picked[:, lat:]], axis=1).astype(bf16)

    load_gain.wait()
    core_out[...] = rows_of(pick_other)

    pl.semaphore_wait(barrier, nx * ny - 1 + nz - 1 + 1)

    for cz in far_z:
        pl.semaphore_signal(plane_sem, inc=1, device_id=device(x, y, cz), device_id_type=MESH)
    swap = pltpu.make_async_remote_copy(
        src_ref=core_out, dst_ref=core_in, send_sem=core_send, recv_sem=core_recv,
        device_id=partner, device_id_type=MESH,
    )
    swap.start()
    load_value.wait()
    swap_value = pltpu.make_async_remote_copy(
        src_ref=value.at[core], dst_ref=value.at[core], send_sem=val_send, recv_sem=val_recv,
        device_id=partner, device_id_type=MESH,
    )
    swap_value.start()

    own_rows = rows_of(pick_own)
    spread = one_hot(iota((2 * chips, chips), 0) == 2 * iota((2 * chips, chips), 1) + (1 - core))
    swap.wait()
    both = own_rows.astype(f32) + dot_nn(spread, core_in[...])
    msg1[...] = both.astype(bf16).reshape(chips, 2, padded)

    def send_row(cx, cy, cz):
        pltpu.make_async_remote_copy(
            src_ref=msg1.at[(cx * ny + cy) * nz + cz], dst_ref=got1.at[chip],
            send_sem=send1, recv_sem=recv1, device_id=device(cx, cy, cz), device_id_type=MESH,
        ).start()

    def send_plane(step, carry):
        cx = moved(x, step, nx)
        for cy in far_y + [y]:
            send_row(cx, cy, z)
        return carry

    lax.fori_loop(0, nx - 1, send_plane, 0)
    for cy in far_y:
        send_row(x, cy, z)

    pl.semaphore_wait(plane_sem, nz - 1)

    def send_slab(step, carry):
        cx = moved(x, step, nx)

        def send_ring(inner, carry):
            cy = moved(y, inner, ny)
            for cz in far_z:
                send_row(cx, cy, cz)
            return carry

        return lax.fori_loop(0, ny, send_ring, carry)

    lax.fori_loop(0, nx, send_slab, 0)
    got1[pl.ds(chip, 1)] = msg1[pl.ds(chip, 1)]

    load_query.wait()
    unit = one_hot(iota((heads, heads), 0) == iota((heads, heads), 1))
    for r in range(2):
        qpad[r * heads : (r + 1) * heads, :] = jnp.concatenate(
            [dot_nt(unit, query_t[r]), jnp.zeros((heads, tail), f32)], axis=1
        ).astype(bf16)
    qpad[2 * heads : 2 * heads + 16, :] = one_hot(
        jnp.logical_and(iota((16, padded), 0) == 0, iota((16, padded), 1) == width)
    )

    load_cache.wait()
    load_len.wait()
    peaks, sums, totals = [], [], []
    for r in range(2):
        scores = dot_nn(qpad[r * heads : (r + 1) * heads, :width], cache[r]) * score_scale
        scores = jnp.where(iota(scores.shape, 1) < len_ref[r], scores, masked)
        peak = jnp.max(scores, axis=1, keepdims=True)
        weight = jnp.exp(scores - peak)
        peaks.append(peak)
        sums.append(jnp.sum(weight, axis=1, keepdims=True))
        totals.append(dot_nt(weight.astype(bf16), cache[r, :lat, :]))
    peak_cache = jnp.concatenate(peaks, axis=0)
    sum_cache = jnp.concatenate(sums, axis=0)
    total_cache = jnp.concatenate(totals, axis=0)

    all_rows = pltpu.make_async_copy(
        msg1.at[pl.ds(0, chips - 1)], got1.at[pl.ds(0, chips - 1)], recv1
    )
    all_rows.wait()
    fresh = got1[...].reshape(2 * chips, padded)
    raw = dot_nt(qpad[...], fresh)
    owner = raw[2 * heads : 2 * heads + 1, :]
    scores = raw[: 2 * heads, :] * score_scale
    row = (iota(scores.shape, 0) // heads).astype(f32)
    scores = jnp.where(row == owner, scores, masked)
    peak = jnp.maximum(peak_cache, jnp.max(scores, axis=1, keepdims=True))
    weight = jnp.exp(scores - peak)
    scale_cache = jnp.exp(peak_cache - peak)
    denominator = sum_cache * scale_cache + jnp.sum(weight, axis=1, keepdims=True)
    total = total_cache * scale_cache + dot_nn(weight.astype(bf16), fresh[:, :lat])
    attended = (total / denominator).astype(bf16)

    line = iota((2 * heads, 2 * heads), 0)
    lane = iota((2 * heads, 2 * heads), 1)
    by_chip = one_hot(lane == ((line // 2) % 2) * heads + (line // 4) * 2 + line % 2)
    msg2[...] = dot_nn(by_chip, attended).astype(bf16).reshape(places, 4, lat)

    def send_heads(cy, cz):
        pltpu.make_async_remote_copy(
            src_ref=msg2.at[cy * nz + cz], dst_ref=got2.at[place],
            send_sem=send2, recv_sem=recv2, device_id=device(x, cy, cz), device_id_type=MESH,
        ).start()

    def send_heads_ring(step, carry):
        cy = moved(y, step, ny)
        for cz in far_z:
            send_heads(cy, cz)
        return carry

    lax.fori_loop(0, ny, send_heads_ring, 0)
    for cy in far_y:
        send_heads(cy, z)
    got2[pl.ds(place, 1)] = msg2[pl.ds(place, 1)]
    swap_value.wait()
    weights = jnp.concatenate([value[0], value[1]], axis=1)
    pltpu.make_async_copy(
        msg2.at[pl.ds(0, places - 1)], got2.at[pl.ds(0, places - 1)], recv2
    ).wait()
    vhead = value.shape[2]
    projected = dot_nn(got2[...].reshape(4 * places, lat), weights)
    even = iota((4 * places, vhead), 0) % 2 == 0
    mine = jnp.where(even, projected[:, :vhead], projected[:, vhead:])
    msg3[...] = mine.astype(bf16).reshape(places, 4, vhead)

    def send_back(cy, cz):
        pltpu.make_async_remote_copy(
            src_ref=msg3.at[cy * nz + cz], dst_ref=got3.at[place],
            send_sem=send3, recv_sem=recv3, device_id=device(x, cy, cz), device_id_type=MESH,
        ).start()

    def send_back_ring(step, carry):
        cy = moved(y, step, ny)
        for cz in far_z:
            send_back(cy, cz)
        return carry

    lax.fori_loop(0, ny, send_back_ring, 0)
    for cy in far_y:
        send_back(cy, z)
    got3[pl.ds(place, 1)] = msg3[pl.ds(place, 1)]
    by_row = one_hot(line == ((lane // 2) % 2) * heads + (lane // 4) * 2 + lane % 2)
    pltpu.make_async_copy(
        msg3.at[pl.ds(0, places - 1)], got3.at[pl.ds(0, places - 1)], recv3
    ).wait()
    out_ref[...] = (
        dot_nn(by_row, got3[...].reshape(4 * places, vhead)).astype(bf16).reshape(2, heads, vhead)
    )

    pltpu.make_async_copy(
        msg1.at[pl.ds(0, chips - 1)], got1.at[pl.ds(0, chips - 1)], send1
    ).wait()
    pltpu.make_async_copy(
        msg2.at[pl.ds(0, places - 1)], got2.at[pl.ds(0, places - 1)], send2
    ).wait()
    pltpu.make_async_copy(
        msg3.at[pl.ds(0, places - 1)], got3.at[pl.ds(0, places - 1)], send3
    ).wait()


def body(kv_pre, kv_gain, send_list, row_owner, queries, cache, ctx_len, value_up):
    nx = lax.axis_size("pool")
    places = lax.axis_size("ep") // 2
    ny = nz = math.isqrt(places)
    chips = nx * places
    lat = kv_gain.shape[0]
    width = kv_pre.shape[1]
    rope = width - lat
    prompt = kv_pre.shape[0]
    rows, heads, _ = queries.shape
    slots = cache.shape[1]
    vhead = value_up.shape[2]
    padded = -(-(width + 1) // 128) * 128

    vmem = pl.BlockSpec(memory_space=pltpu.VMEM)
    hbm = pl.BlockSpec(memory_space=pltpu.HBM)
    dma = pltpu.SemaphoreType.DMA
    return pl.pallas_call(
        functools.partial(kernel, nx, ny, nz, lat, rope),
        out_shape=jax.ShapeDtypeStruct((rows, heads, vhead), bf16),
        in_specs=[hbm] * 8,
        out_specs=vmem,
        scratch_shapes=[
            pltpu.VMEM((1, lat), f32),
            pltpu.VMEM((1, prompt), jnp.int32),
            pltpu.VMEM((1, prompt), jnp.int32),
            pltpu.SMEM((rows,), jnp.int32),
            pltpu.VMEM((padded, prompt), bf16),
            pltpu.VMEM((rows, width, heads), bf16),
            pltpu.VMEM((rows, width, slots), bf16),
            pltpu.VMEM((2, lat, vhead), bf16),
            pltpu.VMEM((rows * heads + 16, padded), bf16),
            pltpu.VMEM((chips, padded), bf16),
            pltpu.VMEM((chips, padded), bf16),
            pltpu.VMEM((chips, 2, padded), bf16),
            pltpu.VMEM((chips, 2, padded), bf16),
            pltpu.VMEM((places, 4, lat), bf16),
            pltpu.VMEM((places, 4, lat), bf16),
            pltpu.VMEM((places, 4, vhead), bf16),
            pltpu.VMEM((places, 4, vhead), bf16),
            dma((8,)),
            dma, dma, dma, dma,
            dma, dma, dma, dma, dma, dma,
            pltpu.SemaphoreType.REGULAR,
        ],
        compiler_params=pltpu.CompilerParams(
            collective_id=0, has_side_effects=True, vmem_limit_bytes=56 * 2**20
        ),
        name="serve_window",
    )(
        kv_gain.reshape(1, lat),
        send_list.reshape(1, prompt),
        row_owner.reshape(1, prompt),
        ctx_len,
        kv_pre.T,
        queries.transpose(0, 2, 1),
        cache.transpose(0, 2, 1),
        value_up,
    )


def solution(mesh):
    in_specs = (
        P(("pool", "ep"), None),
        P(),
        P(("pool", "ep"), None, None),
        P(("pool", "ep")),
        P(("pool", "ep"), None, None),
        P(("pool", "ep"), None, None),
        P(("pool", "ep")),
        P("ep", None, None),
    )
    out_specs = P(("pool", "ep"), None, None)
    return jax.shard_map(body, mesh=mesh, in_specs=in_specs, out_specs=out_specs, check_vma=False)
```

```python
import functools
import math

import jax
import jax.numpy as jnp
import numpy as np
from jax import lax
from jax.experimental import pallas as pl
from jax.experimental.pallas import tpu as pltpu
from jax.sharding import PartitionSpec as P

MESH = pl.DeviceIdType.MESH
score_scale = 192.0 ** (-0.5)
epsilon = 1e-06
f32 = jnp.float32
bf16 = jnp.bfloat16
masked = -1e30


def far_first(step, size):
    if isinstance(step, int):
        return size // 2 + ((step + 1) // 2) * (1 - 2 * (step % 2))
    return size // 2 + lax.div(step + 1, 2) * (1 - 2 * lax.rem(step, 2))


def moved(position, step, size, way):
    place = position + way * far_first(step, size)
    place = jnp.where(place >= size, place - size, place)
    return jnp.where(place < 0, place + size, place)


def dot_nn(a, b):
    return jnp.dot(a, b, preferred_element_type=f32)


def dot_nt(a, b):
    return lax.dot_general(a, b, (((1,), (1,)), ((), ())), preferred_element_type=f32)


def iota(shape, dim):
    return lax.broadcasted_iota(jnp.int32, shape, dim)


def one_hot(condition):
    return jnp.where(condition, 1.0, 0.0).astype(bf16)


def kernel(
    nx, ny, nz, lat, rope,
    gain_hbm, send_hbm, owner_hbm, len_hbm, kv_hbm, query_hbm, cache_hbm, value_hbm,
    out_ref,
    gain_ref, send_ref, owner_ref, len_ref, kv, query_t, cache, value, qpad, core_out, core_in,
    msg1, got1, msg2, got2, msg3, got3,
    load_sem, core_send, core_recv, val_send, val_recv,
    send1, recv1, send2, recv2, send3, recv3, plane_sem,
):
    x = lax.axis_index("pool")
    ep = lax.axis_index("ep")
    y = lax.div(ep, 2 * nz)
    z = lax.div(lax.rem(ep, 2 * nz), 2)
    core = lax.rem(ep, 2)
    way = 1 - 2 * core
    chip = (x * ny + y) * nz + z
    place = y * nz + z
    chips = nx * ny * nz
    places = ny * nz
    prompt = kv.shape[1]
    width = lat + rope
    padded = kv.shape[0]
    heads = query_t.shape[2]
    half = rope // 2
    partner = (x, ep + 1 - 2 * core)

    def device(cx, cy, cz):
        return (cx, (cy * nz + cz) * 2 + core)

    barrier = pltpu.get_barrier_semaphore()

    far_y = [moved(y, step, ny, way) for step in range(ny - 1)]
    far_z = [moved(z, step, nz, way) for step in range(nz - 1)]

    def greet(cx, cy, cz):
        pl.semaphore_signal(barrier, inc=1, device_id=device(cx, cy, cz), device_id_type=MESH)

    def greet_plane(step, carry):
        cx = moved(x, step, nx, way)
        for cy in far_y + [y]:
            greet(cx, cy, z)
        return carry

    lax.fori_loop(0, nx - 1, greet_plane, 0)
    for cy in far_y:
        greet(x, cy, z)
    for cz in far_z:
        greet(x, y, cz)
    pl.semaphore_signal(barrier, inc=1, device_id=partner, device_id_type=MESH)

    load_kv = pltpu.make_async_copy(kv_hbm, kv.at[pl.ds(0, width)], load_sem.at[0])
    load_value = pltpu.make_async_copy(value_hbm.at[0], value.at[core], load_sem.at[1])
    load_query = pltpu.make_async_copy(query_hbm, query_t, load_sem.at[2])
    load_cache = pltpu.make_async_copy(cache_hbm, cache, load_sem.at[3])
    load_gain = pltpu.make_async_copy(gain_hbm, gain_ref, load_sem.at[4])
    load_send = pltpu.make_async_copy(send_hbm, send_ref, load_sem.at[5])
    load_owner = pltpu.make_async_copy(owner_hbm, owner_ref, load_sem.at[6])
    load_len = pltpu.make_async_copy(len_hbm, len_ref, load_sem.at[7])
    load_send.start()
    load_kv.start()
    load_owner.start()
    load_gain.start()
    load_len.start()
    load_value.start()
    load_query.start()
    load_cache.start()

    load_send.wait()
    send_row = send_ref[...].astype(f32)
    lane = iota((chips, prompt), 1)
    line = iota((chips, prompt), 0)
    send_other = jnp.sum(
        jnp.where(lane == 2 * line + (1 - core), send_row, 0.0), axis=1, keepdims=True
    )
    wide_lane = iota((2 * chips, prompt), 1)
    wide_line = iota((2 * chips, prompt), 0)
    send_own = jnp.sum(jnp.where(wide_lane == wide_line, send_row, 0.0), axis=1, keepdims=True)
    pick_other = one_hot(lane.astype(f32) == send_other)
    pick_own = one_hot(
        jnp.logical_and(wide_lane.astype(f32) == send_own, wide_line % 2 == core)
    )

    first_row = ((x * ny + y) * nz + z) * 2 + core
    position = (first_row * prompt + iota((half, prompt), 1)).astype(f32)
    index = iota((half, prompt), 0)
    frequency = jnp.zeros((half, prompt), f32)
    for j in range(half):
        frequency = jnp.where(index == j, float(np.float32(10000.0 ** (-j / half))), frequency)
    angles = position * frequency
    turns = jnp.floor(angles * (1.0 / (2.0 * math.pi)) + 0.5)
    angles = ((angles - turns * 6.28125) - turns * 0.0019340515136718750) - turns * 1.2556659146e-06
    cosine = jnp.cos(angles)
    sine = jnp.sin(angles)
    load_kv.wait()
    first = kv[lat : lat + half, :].astype(f32)
    second = kv[lat + half : width, :].astype(f32)
    kv[lat : lat + half, :] = (first * cosine - second * sine).astype(bf16)
    kv[lat + half : width, :] = (first * sine + second * cosine).astype(bf16)
    tail = padded - width
    load_owner.wait()
    kv[width:padded, :] = jnp.where(
        iota((tail, prompt), 0) == 0, owner_ref[...].astype(f32), 0.0
    ).astype(bf16)

    def rows_of(pick):
        picked = dot_nt(pick, kv[...])
        latent = picked[:, :lat]
        mean_square = jnp.mean(latent * latent, axis=1, keepdims=True)
        normed = latent * lax.rsqrt(mean_square + epsilon) * gain_ref[...]
        return jnp.concatenate([normed, picked[:, lat:]], axis=1).astype(bf16)

    load_gain.wait()
    core_out[...] = rows_of(pick_other)

    pl.semaphore_wait(barrier, nx * ny - 1 + nz - 1 + 1)

    for cz in far_z:
        pl.semaphore_signal(plane_sem, inc=1, device_id=device(x, y, cz), device_id_type=MESH)
    swap = pltpu.make_async_remote_copy(
        src_ref=core_out, dst_ref=core_in, send_sem=core_send, recv_sem=core_recv,
        device_id=partner, device_id_type=MESH,
    )
    swap.start()
    load_value.wait()
    swap_value = pltpu.make_async_remote_copy(
        src_ref=value.at[core], dst_ref=value.at[core], send_sem=val_send, recv_sem=val_recv,
        device_id=partner, device_id_type=MESH,
    )
    swap_value.start()

    own_rows = rows_of(pick_own)
    spread = one_hot(iota((2 * chips, chips), 0) == 2 * iota((2 * chips, chips), 1) + (1 - core))
    swap.wait()
    both = own_rows.astype(f32) + dot_nn(spread, core_in[...])
    msg1[...] = both.astype(bf16).reshape(chips, 2, padded)

    def send_row(cx, cy, cz):
        pltpu.make_async_remote_copy(
            src_ref=msg1.at[(cx * ny + cy) * nz + cz], dst_ref=got1.at[chip],
            send_sem=send1, recv_sem=recv1, device_id=device(cx, cy, cz), device_id_type=MESH,
        ).start()

    def send_plane(step, carry):
        cx = moved(x, step, nx, way)
        for cy in far_y + [y]:
            send_row(cx, cy, z)
        return carry

    lax.fori_loop(0, nx - 1, send_plane, 0)
    for cy in far_y:
        send_row(x, cy, z)

    pl.semaphore_wait(plane_sem, nz - 1)

    def send_slab(step, carry):
        cx = moved(x, step, nx, way)

        def send_ring(inner, carry):
            cy = moved(y, inner, ny, way)
            for cz in far_z:
                send_row(cx, cy, cz)
            return carry

        return lax.fori_loop(0, ny, send_ring, carry)

    lax.fori_loop(0, nx, send_slab, 0)
    got1[pl.ds(chip, 1)] = msg1[pl.ds(chip, 1)]

    load_query.wait()
    unit = one_hot(iota((heads, heads), 0) == iota((heads, heads), 1))
    for r in range(2):
        qpad[r * heads : (r + 1) * heads, :] = jnp.concatenate(
            [dot_nt(unit, query_t[r]), jnp.zeros((heads, tail), f32)], axis=1
        ).astype(bf16)
    qpad[2 * heads : 2 * heads + 16, :] = one_hot(
        jnp.logical_and(iota((16, padded), 0) == 0, iota((16, padded), 1) == width)
    )

    load_cache.wait()
    load_len.wait()
    peaks, sums, totals = [], [], []
    for r in range(2):
        scores = dot_nn(qpad[r * heads : (r + 1) * heads, :width], cache[r]) * score_scale
        scores = jnp.where(iota(scores.shape, 1) < len_ref[r], scores, masked)
        peak = jnp.max(scores, axis=1, keepdims=True)
        weight = jnp.exp(scores - peak)
        peaks.append(peak)
        sums.append(jnp.sum(weight, axis=1, keepdims=True))
        totals.append(dot_nt(weight.astype(bf16), cache[r, :lat, :]))
    peak_cache = jnp.concatenate(peaks, axis=0)
    sum_cache = jnp.concatenate(sums, axis=0)
    total_cache = jnp.concatenate(totals, axis=0)

    all_rows = pltpu.make_async_copy(
        msg1.at[pl.ds(0, chips - 1)], got1.at[pl.ds(0, chips - 1)], recv1
    )
    all_rows.wait()
    fresh = got1[...].reshape(2 * chips, padded)
    raw = dot_nt(qpad[...], fresh)
    owner = raw[2 * heads : 2 * heads + 1, :]
    scores = raw[: 2 * heads, :] * score_scale
    row = (iota(scores.shape, 0) // heads).astype(f32)
    scores = jnp.where(row == owner, scores, masked)
    peak = jnp.maximum(peak_cache, jnp.max(scores, axis=1, keepdims=True))
    weight = jnp.exp(scores - peak)
    scale_cache = jnp.exp(peak_cache - peak)
    denominator = sum_cache * scale_cache + jnp.sum(weight, axis=1, keepdims=True)
    total = total_cache * scale_cache + dot_nn(weight.astype(bf16), fresh[:, :lat])
    attended = (total / denominator).astype(bf16)

    line = iota((2 * heads, 2 * heads), 0)
    lane = iota((2 * heads, 2 * heads), 1)
    by_chip = one_hot(lane == ((line // 2) % 2) * heads + (line // 4) * 2 + line % 2)
    msg2[...] = dot_nn(by_chip, attended).astype(bf16).reshape(places, 4, lat)

    groups = [(0, 3), (3, ny - 3), (ny - 3, ny)] if ny == 8 else [(0, ny)]

    def exchange(group, source, target, send_sem, recv_sem):
        def send(cy, cz):
            pltpu.make_async_remote_copy(
                src_ref=source.at[cy * nz + cz], dst_ref=target.at[place],
                send_sem=send_sem, recv_sem=recv_sem.at[group],
                device_id=device(x, cy, cz), device_id_type=MESH,
            ).start()

        def send_ring(step, carry):
            cy = moved(y, step, ny, way)
            for cz in far_z + [z]:
                send(cy, cz)
            return carry

        start, stop = groups[group]
        last = stop == ny
        lax.fori_loop(start, stop - 1 if last else stop, send_ring, 0)
        if last:
            for cz in far_z:
                send(y, cz)
            target[pl.ds(place, 1)] = source[pl.ds(place, 1)]

    def arrival(group, source, target, recv_sem):
        start, stop = groups[group]
        count = (stop - start) * nz - (1 if stop == ny else 0)
        pltpu.make_async_copy(
            source.at[pl.ds(0, count)], target.at[pl.ds(0, count)], recv_sem.at[group]
        ).wait()

    for group in range(len(groups)):
        exchange(group, msg2, got2, send2, recv2)
    swap_value.wait()
    weights = jnp.concatenate([value[0], value[1]], axis=1)
    vhead = value.shape[2]
    for group in range(len(groups)):
        arrival(group, msg2, got2, recv2)
        rings = [moved(y, step, ny, way) for step in range(*groups[group])]
        arrived = jnp.concatenate(
            [got2[pl.ds(cy * nz, nz)].reshape(4 * nz, lat) for cy in rings], axis=0
        )
        projected = dot_nn(arrived, weights)
        even = lax.rem(iota((arrived.shape[0], vhead), 0), 2) == 0
        mine = jnp.where(even, projected[:, :vhead], projected[:, vhead:])
        mine = mine.astype(bf16).reshape(len(rings) * nz, 4, vhead)
        for index, cy in enumerate(rings):
            msg3[pl.ds(cy * nz, nz)] = mine[index * nz : (index + 1) * nz]
        exchange(group, msg3, got3, send3, recv3)

    by_row = one_hot(line == ((lane // 2) % 2) * heads + (lane // 4) * 2 + lane % 2)
    for group in range(len(groups)):
        arrival(group, msg3, got3, recv3)
    out_ref[...] = (
        dot_nn(by_row, got3[...].reshape(4 * places, vhead)).astype(bf16).reshape(2, heads, vhead)
    )

    pltpu.make_async_copy(
        msg1.at[pl.ds(0, chips - 1)], got1.at[pl.ds(0, chips - 1)], send1
    ).wait()
    pltpu.make_async_copy(
        msg2.at[pl.ds(0, places - 1)], got2.at[pl.ds(0, places - 1)], send2
    ).wait()
    pltpu.make_async_copy(
        msg3.at[pl.ds(0, places - 1)], got3.at[pl.ds(0, places - 1)], send3
    ).wait()


def body(kv_pre, kv_gain, send_list, row_owner, queries, cache, ctx_len, value_up):
    nx = lax.axis_size("pool")
    places = lax.axis_size("ep") // 2
    ny = nz = math.isqrt(places)
    chips = nx * places
    lat = kv_gain.shape[0]
    width = kv_pre.shape[1]
    rope = width - lat
    prompt = kv_pre.shape[0]
    rows, heads, _ = queries.shape
    slots = cache.shape[1]
    vhead = value_up.shape[2]
    padded = -(-(width + 1) // 128) * 128

    vmem = pl.BlockSpec(memory_space=pltpu.VMEM)
    hbm = pl.BlockSpec(memory_space=pltpu.HBM)
    dma = pltpu.SemaphoreType.DMA
    return pl.pallas_call(
        functools.partial(kernel, nx, ny, nz, lat, rope),
        out_shape=jax.ShapeDtypeStruct((rows, heads, vhead), bf16),
        in_specs=[hbm] * 8,
        out_specs=vmem,
        scratch_shapes=[
            pltpu.VMEM((1, lat), f32),
            pltpu.VMEM((1, prompt), jnp.int32),
            pltpu.VMEM((1, prompt), jnp.int32),
            pltpu.SMEM((rows,), jnp.int32),
            pltpu.VMEM((padded, prompt), bf16),
            pltpu.VMEM((rows, width, heads), bf16),
            pltpu.VMEM((rows, width, slots), bf16),
            pltpu.VMEM((2, lat, vhead), bf16),
            pltpu.VMEM((rows * heads + 16, padded), bf16),
            pltpu.VMEM((chips, padded), bf16),
            pltpu.VMEM((chips, padded), bf16),
            pltpu.VMEM((chips, 2, padded), bf16),
            pltpu.VMEM((chips, 2, padded), bf16),
            pltpu.VMEM((places, 4, lat), bf16),
            pltpu.VMEM((places, 4, lat), bf16),
            pltpu.VMEM((places, 4, vhead), bf16),
            pltpu.VMEM((places, 4, vhead), bf16),
            dma((8,)),
            dma, dma, dma, dma,
            dma, dma, dma, dma((3,)), dma, dma((3,)),
            pltpu.SemaphoreType.REGULAR,
        ],
        compiler_params=pltpu.CompilerParams(
            collective_id=0, has_side_effects=True, vmem_limit_bytes=56 * 2**20
        ),
        name="serve_window",
    )(
        kv_gain.reshape(1, lat),
        send_list.reshape(1, prompt),
        row_owner.reshape(1, prompt),
        ctx_len,
        kv_pre.T,
        queries.transpose(0, 2, 1),
        cache.transpose(0, 2, 1),
        value_up,
    )


def solution(mesh):
    in_specs = (
        P(("pool", "ep"), None),
        P(),
        P(("pool", "ep"), None, None),
        P(("pool", "ep")),
        P(("pool", "ep"), None, None),
        P(("pool", "ep"), None, None),
        P(("pool", "ep")),
        P("ep", None, None),
    )
    out_specs = P(("pool", "ep"), None, None)
    return jax.shard_map(body, mesh=mesh, in_specs=in_specs, out_specs=out_specs, check_vma=False)
```

```python
import functools
import math

import jax
import jax.numpy as jnp
import numpy as np
from jax import lax
from jax.experimental import pallas as pl
from jax.experimental.pallas import tpu as pltpu
from jax.sharding import PartitionSpec as P

MESH = pl.DeviceIdType.MESH
score_scale = 192.0 ** (-0.5)
epsilon = 1e-06
f32 = jnp.float32
bf16 = jnp.bfloat16
masked = -1e30


def far_first(step, size):
    if isinstance(step, int):
        return size // 2 + ((step + 1) // 2) * (1 - 2 * (step % 2))
    return size // 2 + lax.div(step + 1, 2) * (1 - 2 * lax.rem(step, 2))


def moved(position, step, size, way):
    place = position + way * far_first(step, size)
    place = jnp.where(place >= size, place - size, place)
    return jnp.where(place < 0, place + size, place)


def dot_nn(a, b):
    return jnp.dot(a, b, preferred_element_type=f32)


def dot_nt(a, b):
    return lax.dot_general(a, b, (((1,), (1,)), ((), ())), preferred_element_type=f32)


def iota(shape, dim):
    return lax.broadcasted_iota(jnp.int32, shape, dim)


def one_hot(condition):
    return jnp.where(condition, 1.0, 0.0).astype(bf16)


def kernel(
    nx, ny, nz, lat, rope,
    gain_hbm, send_hbm, owner_hbm, len_hbm, kv_hbm, query_hbm, cache_hbm, value_hbm,
    out_ref,
    gain_ref, send_ref, owner_ref, len_ref, kv, query_t, cache, value, qpad, core_out, core_in,
    msg1, got1, msg2, got2, msg3, got3,
    load_sem, core_send, core_recv, val_send, val_recv,
    send1, recv1, send2, recv2, send3, recv3, plane_sem,
):
    x = lax.axis_index("pool")
    ep = lax.axis_index("ep")
    y = lax.div(ep, 2 * nz)
    z = lax.div(lax.rem(ep, 2 * nz), 2)
    core = lax.rem(ep, 2)
    way = 1 - 2 * core
    chip = (x * ny + y) * nz + z
    place = y * nz + z
    chips = nx * ny * nz
    places = ny * nz
    prompt = kv.shape[1]
    width = lat + rope
    padded = kv.shape[0]
    heads = query_t.shape[2]
    half = rope // 2
    partner = (x, ep + 1 - 2 * core)

    def device(cx, cy, cz):
        return (cx, (cy * nz + cz) * 2 + core)

    barrier = pltpu.get_barrier_semaphore()

    far_y = [moved(y, step, ny, way) for step in range(ny - 1)]
    far_z = [moved(z, step, nz, way) for step in range(nz - 1)]

    def greet(cx, cy, cz):
        pl.semaphore_signal(barrier, inc=1, device_id=device(cx, cy, cz), device_id_type=MESH)

    def greet_plane(step, carry):
        cx = moved(x, step, nx, way)
        for cy in far_y + [y]:
            greet(cx, cy, z)
        return carry

    lax.fori_loop(0, nx - 1, greet_plane, 0)
    for cy in far_y:
        greet(x, cy, z)
    for cz in far_z:
        greet(x, y, cz)
    pl.semaphore_signal(barrier, inc=1, device_id=partner, device_id_type=MESH)

    load_kv = pltpu.make_async_copy(kv_hbm, kv.at[pl.ds(0, width)], load_sem.at[0])
    load_value = pltpu.make_async_copy(value_hbm.at[0], value.at[core], load_sem.at[1])
    load_query = pltpu.make_async_copy(query_hbm, query_t, load_sem.at[2])
    load_cache = pltpu.make_async_copy(cache_hbm, cache, load_sem.at[3])
    load_gain = pltpu.make_async_copy(gain_hbm, gain_ref, load_sem.at[4])
    load_send = pltpu.make_async_copy(send_hbm, send_ref, load_sem.at[5])
    load_owner = pltpu.make_async_copy(owner_hbm, owner_ref, load_sem.at[6])
    load_len = pltpu.make_async_copy(len_hbm, len_ref, load_sem.at[7])
    load_send.start()
    load_kv.start()
    load_owner.start()
    load_gain.start()
    load_len.start()
    load_value.start()
    load_query.start()
    load_cache.start()

    load_send.wait()
    send_row = send_ref[...].astype(f32)
    lane = iota((chips, prompt), 1)
    line = iota((chips, prompt), 0)
    send_other = jnp.sum(
        jnp.where(lane == 2 * line + (1 - core), send_row, 0.0), axis=1, keepdims=True
    )
    wide_lane = iota((2 * chips, prompt), 1)
    wide_line = iota((2 * chips, prompt), 0)
    send_own = jnp.sum(jnp.where(wide_lane == wide_line, send_row, 0.0), axis=1, keepdims=True)
    pick_other = one_hot(lane.astype(f32) == send_other)
    pick_own = one_hot(
        jnp.logical_and(wide_lane.astype(f32) == send_own, wide_line % 2 == core)
    )

    first_row = ((x * ny + y) * nz + z) * 2 + core
    position = (first_row * prompt + iota((half, prompt), 1)).astype(f32)
    index = iota((half, prompt), 0)
    frequency = jnp.zeros((half, prompt), f32)
    for j in range(half):
        frequency = jnp.where(index == j, float(np.float32(10000.0 ** (-j / half))), frequency)
    angles = position * frequency
    turns = jnp.floor(angles * (1.0 / (2.0 * math.pi)) + 0.5)
    angles = ((angles - turns * 6.28125) - turns * 0.0019340515136718750) - turns * 1.2556659146e-06
    cosine = jnp.cos(angles)
    sine = jnp.sin(angles)
    load_kv.wait()
    first = kv[lat : lat + half, :].astype(f32)
    second = kv[lat + half : width, :].astype(f32)
    kv[lat : lat + half, :] = (first * cosine - second * sine).astype(bf16)
    kv[lat + half : width, :] = (first * sine + second * cosine).astype(bf16)
    tail = padded - width
    load_owner.wait()
    kv[width:padded, :] = jnp.where(
        iota((tail, prompt), 0) == 0, owner_ref[...].astype(f32), 0.0
    ).astype(bf16)

    def rows_of(pick):
        picked = dot_nt(pick, kv[...])
        latent = picked[:, :lat]
        mean_square = jnp.mean(latent * latent, axis=1, keepdims=True)
        normed = latent * lax.rsqrt(mean_square + epsilon) * gain_ref[...]
        return jnp.concatenate([normed, picked[:, lat:]], axis=1).astype(bf16)

    load_gain.wait()
    core_out[...] = rows_of(pick_other)

    pl.semaphore_wait(barrier, nx * ny - 1 + nz - 1 + 1)

    for cz in far_z:
        pl.semaphore_signal(plane_sem, inc=1, device_id=device(x, y, cz), device_id_type=MESH)
    swap = pltpu.make_async_remote_copy(
        src_ref=core_out, dst_ref=core_in, send_sem=core_send, recv_sem=core_recv,
        device_id=partner, device_id_type=MESH,
    )
    swap.start()
    load_value.wait()
    swap_value = pltpu.make_async_remote_copy(
        src_ref=value.at[core], dst_ref=value.at[core], send_sem=val_send, recv_sem=val_recv,
        device_id=partner, device_id_type=MESH,
    )
    swap_value.start()

    own_rows = rows_of(pick_own)
    spread = one_hot(iota((2 * chips, chips), 0) == 2 * iota((2 * chips, chips), 1) + (1 - core))
    swap.wait()
    both = own_rows.astype(f32) + dot_nn(spread, core_in[...])
    msg1[...] = both.astype(bf16).reshape(chips, 2, padded)

    def send_row(cx, cy, cz, near):
        pltpu.make_async_remote_copy(
            src_ref=msg1.at[(cx * ny + cy) * nz + cz], dst_ref=got1.at[chip],
            send_sem=send1, recv_sem=recv1.at[near], device_id=device(cx, cy, cz), device_id_type=MESH,
        ).start()

    def send_plane(step, carry):
        cx = moved(x, step, nx, way)
        for cy in far_y + [y]:
            send_row(cx, cy, z, 0)
        return carry

    lax.fori_loop(0, nx - 1, send_plane, 0)
    for cy in far_y:
        send_row(x, cy, z, 1)

    pl.semaphore_wait(plane_sem, nz - 1)

    def send_slab(cx, near):
        def send_ring(inner, carry):
            cy = moved(y, inner, ny, way)
            for cz in far_z:
                send_row(cx, cy, cz, near)
            return carry

        lax.fori_loop(0, ny, send_ring, 0)

    def send_far_slab(step, carry):
        send_slab(moved(x, step, nx, way), 0)
        return carry

    lax.fori_loop(0, nx - 1, send_far_slab, 0)
    send_slab(x, 1)
    got1[pl.ds(chip, 1)] = msg1[pl.ds(chip, 1)]

    load_query.wait()
    unit = one_hot(iota((heads, heads), 0) == iota((heads, heads), 1))
    line = iota((2 * heads, 2 * heads), 0)
    lane = iota((2 * heads, 2 * heads), 1)
    by_chip = one_hot(
        lane == lax.rem(lax.div(line, 2), 2) * heads + lax.div(line, 4) * 2 + lax.rem(line, 2)
    )
    query = [dot_nt(unit, query_t[r]).astype(bf16) for r in range(2)]
    ordered = dot_nn(by_chip, jnp.concatenate(query, axis=0))
    qpad[: 2 * heads, :] = jnp.concatenate(
        [ordered, jnp.zeros((2 * heads, tail), f32)], axis=1
    ).astype(bf16)
    qpad[2 * heads : 2 * heads + 16, :] = one_hot(
        jnp.logical_and(iota((16, padded), 0) == 0, iota((16, padded), 1) == width)
    )

    load_cache.wait()
    load_len.wait()
    peaks, sums, totals = [], [], []
    for r in range(2):
        scores = dot_nn(query[r], cache[r]) * score_scale
        scores = jnp.where(iota(scores.shape, 1) < len_ref[r], scores, masked)
        peak = jnp.max(scores, axis=1, keepdims=True)
        weight = jnp.exp(scores - peak)
        peaks.append(peak)
        sums.append(jnp.sum(weight, axis=1, keepdims=True))
        totals.append(dot_nt(weight.astype(bf16), cache[r, :lat, :]))
    side = jnp.where(
        iota((2 * heads, 128), 1) == 0,
        jnp.concatenate(peaks, axis=0),
        jnp.concatenate(sums, axis=0),
    )
    held = jnp.dot(
        by_chip.astype(f32),
        jnp.concatenate([jnp.concatenate(totals, axis=0), side], axis=1),
        precision=lax.Precision.HIGHEST,
        preferred_element_type=f32,
    )
    total_cache = held[:, :lat]
    peak_cache = held[:, lat : lat + 1]
    sum_cache = held[:, lat + 1 : lat + 2]

    far_count = (nx - 1) * places
    pltpu.make_async_copy(
        msg1.at[pl.ds(0, far_count)], got1.at[pl.ds(0, far_count)], recv1.at[0]
    ).wait()
    slabs = [lax.rem(x + step, nx) for step in range(1, nx)]
    far_keys = jnp.concatenate(
        [got1[pl.ds(cx * places, places)].reshape(2 * places, padded) for cx in slabs], axis=0
    )
    far_raw = dot_nt(qpad[...], far_keys)
    pltpu.make_async_copy(
        msg1.at[pl.ds(0, places - 1)], got1.at[pl.ds(0, places - 1)], recv1.at[1]
    ).wait()
    near_keys = got1[pl.ds(x * places, places)].reshape(2 * places, padded)
    raw = jnp.concatenate([far_raw, dot_nt(qpad[...], near_keys)], axis=1)
    owner = raw[2 * heads : 2 * heads + 1, :]
    scores = raw[: 2 * heads, :] * score_scale
    row = lax.rem(lax.div(iota(scores.shape, 0), 2), 2).astype(f32)
    scores = jnp.where(row == owner, scores, masked)
    peak = jnp.maximum(peak_cache, jnp.max(scores, axis=1, keepdims=True))
    weight = jnp.exp(scores - peak)
    scale_cache = jnp.exp(peak_cache - peak)
    denominator = sum_cache * scale_cache + jnp.sum(weight, axis=1, keepdims=True)
    weight = weight.astype(bf16)
    split = 2 * far_count
    total = (
        total_cache * scale_cache
        + dot_nn(weight[:, :split], far_keys[:, :lat])
        + dot_nn(weight[:, split:], near_keys[:, :lat])
    )

    msg2[...] = (total / denominator).astype(bf16).reshape(places, 4, lat)

    groups = [(0, 3), (3, ny - 3), (ny - 3, ny)] if ny == 8 else [(0, ny)]

    def exchange(group, source, target, send_sem, recv_sem):
        def send(cy, cz):
            pltpu.make_async_remote_copy(
                src_ref=source.at[cy * nz + cz], dst_ref=target.at[place],
                send_sem=send_sem, recv_sem=recv_sem.at[group],
                device_id=device(x, cy, cz), device_id_type=MESH,
            ).start()

        def send_ring(step, carry):
            cy = moved(y, step, ny, way)
            for cz in far_z + [z]:
                send(cy, cz)
            return carry

        start, stop = groups[group]
        last = stop == ny
        lax.fori_loop(start, stop - 1 if last else stop, send_ring, 0)
        if last:
            for cz in far_z:
                send(y, cz)
            target[pl.ds(place, 1)] = source[pl.ds(place, 1)]

    def arrival(group, source, target, recv_sem):
        start, stop = groups[group]
        count = (stop - start) * nz - (1 if stop == ny else 0)
        pltpu.make_async_copy(
            source.at[pl.ds(0, count)], target.at[pl.ds(0, count)], recv_sem.at[group]
        ).wait()

    for group in range(len(groups)):
        exchange(group, msg2, got2, send2, recv2)
    swap_value.wait()
    weights = jnp.concatenate([value[0], value[1]], axis=1)
    vhead = value.shape[2]
    for group in range(len(groups)):
        arrival(group, msg2, got2, recv2)
        rings = [moved(y, step, ny, way) for step in range(*groups[group])]
        arrived = jnp.concatenate(
            [got2[pl.ds(cy * nz, nz)].reshape(4 * nz, lat) for cy in rings], axis=0
        )
        projected = dot_nn(arrived, weights)
        even = lax.rem(iota((arrived.shape[0], vhead), 0), 2) == 0
        mine = jnp.where(even, projected[:, :vhead], projected[:, vhead:])
        mine = mine.astype(bf16).reshape(len(rings) * nz, 4, vhead)
        for index, cy in enumerate(rings):
            msg3[pl.ds(cy * nz, nz)] = mine[index * nz : (index + 1) * nz]
        exchange(group, msg3, got3, send3, recv3)

    by_row = one_hot(line == ((lane // 2) % 2) * heads + (lane // 4) * 2 + lane % 2)
    for group in range(len(groups)):
        arrival(group, msg3, got3, recv3)
    out_ref[...] = (
        dot_nn(by_row, got3[...].reshape(4 * places, vhead)).astype(bf16).reshape(2, heads, vhead)
    )

    pltpu.make_async_copy(
        msg1.at[pl.ds(0, chips - 1)], got1.at[pl.ds(0, chips - 1)], send1
    ).wait()
    pltpu.make_async_copy(
        msg2.at[pl.ds(0, places - 1)], got2.at[pl.ds(0, places - 1)], send2
    ).wait()
    pltpu.make_async_copy(
        msg3.at[pl.ds(0, places - 1)], got3.at[pl.ds(0, places - 1)], send3
    ).wait()


def body(kv_pre, kv_gain, send_list, row_owner, queries, cache, ctx_len, value_up):
    nx = lax.axis_size("pool")
    places = lax.axis_size("ep") // 2
    ny = nz = math.isqrt(places)
    chips = nx * places
    lat = kv_gain.shape[0]
    width = kv_pre.shape[1]
    rope = width - lat
    prompt = kv_pre.shape[0]
    rows, heads, _ = queries.shape
    slots = cache.shape[1]
    vhead = value_up.shape[2]
    padded = -(-(width + 1) // 128) * 128

    vmem = pl.BlockSpec(memory_space=pltpu.VMEM)
    hbm = pl.BlockSpec(memory_space=pltpu.HBM)
    dma = pltpu.SemaphoreType.DMA
    return pl.pallas_call(
        functools.partial(kernel, nx, ny, nz, lat, rope),
        out_shape=jax.ShapeDtypeStruct((rows, heads, vhead), bf16),
        in_specs=[hbm] * 8,
        out_specs=vmem,
        scratch_shapes=[
            pltpu.VMEM((1, lat), f32),
            pltpu.VMEM((1, prompt), jnp.int32),
            pltpu.VMEM((1, prompt), jnp.int32),
            pltpu.SMEM((rows,), jnp.int32),
            pltpu.VMEM((padded, prompt), bf16),
            pltpu.VMEM((rows, width, heads), bf16),
            pltpu.VMEM((rows, width, slots), bf16),
            pltpu.VMEM((2, lat, vhead), bf16),
            pltpu.VMEM((rows * heads + 16, padded), bf16),
            pltpu.VMEM((chips, padded), bf16),
            pltpu.VMEM((chips, padded), bf16),
            pltpu.VMEM((chips, 2, padded), bf16),
            pltpu.VMEM((chips, 2, padded), bf16),
            pltpu.VMEM((places, 4, lat), bf16),
            pltpu.VMEM((places, 4, lat), bf16),
            pltpu.VMEM((places, 4, vhead), bf16),
            pltpu.VMEM((places, 4, vhead), bf16),
            dma((8,)),
            dma, dma, dma, dma,
            dma, dma((2,)), dma, dma((3,)), dma, dma((3,)),
            pltpu.SemaphoreType.REGULAR,
        ],
        compiler_params=pltpu.CompilerParams(
            collective_id=0, has_side_effects=True, vmem_limit_bytes=56 * 2**20
        ),
        name="serve_window",
    )(
        kv_gain.reshape(1, lat),
        send_list.reshape(1, prompt),
        row_owner.reshape(1, prompt),
        ctx_len,
        kv_pre.T,
        queries.transpose(0, 2, 1),
        cache.transpose(0, 2, 1),
        value_up,
    )


def solution(mesh):
    in_specs = (
        P(("pool", "ep"), None),
        P(),
        P(("pool", "ep"), None, None),
        P(("pool", "ep")),
        P(("pool", "ep"), None, None),
        P(("pool", "ep"), None, None),
        P(("pool", "ep")),
        P("ep", None, None),
    )
    out_specs = P(("pool", "ep"), None, None)
    return jax.shard_map(body, mesh=mesh, in_specs=in_specs, out_specs=out_specs, check_vma=False)
```
